32 devices in a mesh: outer: 4 (over y, x), inner: 8 (over z, core).
Axes of the slice: x: 2, y: 2, z: 4, core: 2. Of those that a mesh axis runs over, the one named last changes fastest.
Arguments:
- points: float32 [3584, 256], P(('outer', 'inner')), may hold values from -36 to 36
- vectors: float32 [3584, 128], P(('outer', 'inner')), may hold values from -6 to 6
- lengthscales: float32 [256], replicated, may hold values from 8 to 32
- outputscale: float32 [1], replicated, may hold values from 0.03 to 0.12
- noise: float32 [1], replicated, may hold values from 0.3 to 3
Outputs:
- product: float32 [3584, 128], P(('outer', 'inner'))
The draws below stay inside these ranges and needn't reach their ends.
All inputs are finite; a program needn't handle non-finite values.
Results may differ from the reference program's by a relative error of at most 0.00024.
Values sent between devices are 32-bit elements; how exact they have to be, the bound alone decides.
No kernel may reach another device: no remote copies, remote signals or barrier semaphores. Data moves between devices by JAX's collectives and lax.ppermute only.
A program may use at most 128 MiB of HBM per device.

```python
import math
import jax
import jax.numpy as jnp
from jax import lax

P_DEV = 112
F = 256
R = 128
N = 3584


def draw_points(key, part):
    key_center, key_member, key_latent, key_basis, key_noise = jax.random.split(jax.random.fold_in(key, 7), 5)
    member = jax.random.randint(key_member, (N,), 0, 32)
    one_hot = (member[:, None] == jnp.arange(32)[None, :]).astype(jnp.float32)
    basis = jax.random.uniform(key_basis, (8, F), jnp.float32, -1.0, 1.0) * math.sqrt(3.0 / 8.0)
    centers = 0.9 * jax.random.truncated_normal(key_center, -3.0, 3.0, (32, 8), jnp.float32)
    latent = 0.4 * jax.random.truncated_normal(key_latent, -3.0, 3.0, (N, 8), jnp.float32)
    jitter = 1.2 * jax.random.truncated_normal(key_noise, -3.0, 3.0, (N, F), jnp.float32)
    coords = jnp.dot(one_hot, centers, precision=lax.Precision.HIGHEST) + latent
    return jnp.dot(coords, basis, precision=lax.Precision.HIGHEST) + jitter


def block_scale(rng, shape, pieces, smallest, high):
    def one(dim, blocks):
        draws = jax.random.uniform(jax.random.fold_in(jax.random.fold_in(rng, 6), dim), (blocks,), jnp.float32, smallest / len(pieces), high / len(pieces))
        return jnp.repeat(jnp.exp(draws), shape[dim] // blocks).reshape((-1,) + (1,) * (len(shape) - dim - 1))

    gain = one(*pieces[0])
    for cut in pieces[1:]:
        gain = gain * one(*cut)
    return gain


def centred(rng, dims, spread, bound, shards=(), kind=jnp.bfloat16):
    entries = jax.random.normal(rng, dims, jnp.float32) * spread
    if len(shards) > 0:
        entries = block_scale(rng, dims, shards, -0.22, 0.18) * entries
    return jnp.clip(entries, min=-bound, max=bound).astype(kind)


def setup_inputs(seed: int = 0) -> dict:
    key_list = jax.random.split(jax.random.key(seed), 6)
    points = draw_points(jax.random.fold_in(key_list[5], 71), 0)
    vectors = centred(key_list[1], (N, R), 1.0, 6.0, ((0, 32),), jnp.float32)
    lengthscales = jnp.clip(jnp.exp(jax.random.uniform(key_list[2], (F,), jnp.float32, math.log(8.0), math.log(32.0))), 8.0, 32.0)
    outputscale = jnp.clip(jnp.exp(jax.random.uniform(key_list[3], (1,), jnp.float32, math.log(0.03), math.log(0.12))), 0.03, 0.12)
    noise = jnp.clip(jnp.exp(jax.random.uniform(key_list[4], (1,), jnp.float32, math.log(0.3), math.log(3.0))), 0.3, 3.0)
    return {"points": points, "vectors": vectors, "lengthscales": lengthscales, "outputscale": outputscale, "noise": noise}


def matern(dist2, amplitude):
    scaled_r = jnp.sqrt(5.0) * jnp.sqrt(jnp.maximum(dist2, 0.0))
    return amplitude * (1.0 + scaled_r + scaled_r * scaled_r / 3.0) * jnp.exp(-scaled_r)

def reference(points, vectors, lengthscales, outputscale, noise):
    scaled = points / lengthscales[None, :]
    sqnorm = lax.optimization_barrier(jnp.sum(scaled * scaled, axis=1))
    blocks = N // 512 if N % 512 == 0 else N // P_DEV
    rows_block = N // blocks
    row_sets = scaled.reshape(blocks, rows_block, F)
    norm_sets = sqnorm.reshape(blocks, rows_block)

    def one_block(pair):
        rows, norms = pair
        inner_prod = jnp.dot(rows, scaled.T, precision=lax.Precision.HIGHEST, preferred_element_type=jnp.float32)
        dist2 = norms[:, None] + sqnorm[None, :] - 2.0 * inner_prod
        kernel = matern(dist2, outputscale[0])
        return jnp.dot(kernel, vectors, precision=lax.Precision.HIGHEST, preferred_element_type=jnp.float32)
    product = lax.map(one_block, (row_sets, norm_sets)).reshape(N, R)
    return product + noise[0] * vectors
```

```python
import jax
import jax.numpy as jnp
from jax import lax
from jax.sharding import PartitionSpec as P

AXES = ("outer", "inner")
CORES = 2


def matern(dist2, amplitude):
    scaled_r = jnp.sqrt(5.0) * jnp.sqrt(jnp.maximum(dist2, 0.0))
    return amplitude * (1.0 + scaled_r + scaled_r * scaled_r / 3.0) * jnp.exp(-scaled_r)


def row_norms(rows):
    return jnp.sum(rows * rows, axis=1)


def partner(index, step, size):
    return index ^ step if size & (size - 1) == 0 else (index + step) % size


def solution(mesh):
    n_outer, n_inner = mesh.shape["outer"], mesh.shape["inner"]
    n_line = n_inner // CORES

    def linear(outer, line, core):
        return outer * n_inner + line * CORES + core

    places = [(o, z, c) for o in range(n_outer) for z in range(n_line) for c in range(CORES)]

    def along_line(step):
        return [(linear(o, z, c), linear(o, partner(z, step, n_line), c)) for o, z, c in places]

    def along_outer(step):
        return [(linear(o, z, c), linear(partner(o, step, n_outer), z, c)) for o, z, c in places]

    other_core = [(linear(o, z, c), linear(o, z, c ^ 1)) for o, z, c in places]

    def per_device(points, vectors, lengthscales, outputscale, noise):
        here = points.shape[0]
        features = points.shape[1]
        row_blocks = [points] + [lax.ppermute(points, AXES, along_line(k)) for k in range(1, n_line)]
        both = jnp.concatenate([points, vectors], axis=1)
        col_blocks = [both] + [lax.ppermute(both, AXES, along_outer(k)) for k in range(1, n_outer)]
        cols_mine = jnp.concatenate(col_blocks, axis=0)
        cols_theirs = lax.ppermute(cols_mine, AXES, other_core)
        cols = jnp.concatenate([cols_mine, cols_theirs], axis=0)
        rows = jnp.concatenate(row_blocks, axis=0) / lengthscales[None, :]
        values = cols[:, features:]
        cols = cols[:, :features] / lengthscales[None, :]
        inner_prod = jnp.dot(rows, cols.T, precision=lax.Precision.HIGHEST, preferred_element_type=jnp.float32)
        dist2 = row_norms(rows)[:, None] + row_norms(cols)[None, :] - 2.0 * inner_prod
        tile = matern(dist2, outputscale[0])
        partial = jnp.dot(tile, values, precision=lax.Precision.HIGHEST, preferred_element_type=jnp.float32)
        total = partial[:here] + noise[0] * vectors
        for k in range(1, n_line):
            back = [(b, a) for a, b in along_line(k)]
            total = total + lax.ppermute(partial[k * here : (k + 1) * here], AXES, back)
        return total

    placed = (P(AXES, None), P(AXES, None), P(), P(), P())
    return jax.shard_map(per_device, mesh=mesh, in_specs=placed, out_specs=P(AXES, None), check_vma=False)
```

```python
import functools

import jax
import jax.numpy as jnp
from jax import lax
from jax.experimental import pallas as pl
from jax.experimental.pallas import tpu as pltpu
from jax.sharding import PartitionSpec as P

AXES = ("outer", "inner")
CORES = 2
VMEM = pl.BlockSpec(memory_space=pltpu.VMEM)
SMEM = pl.BlockSpec(memory_space=pltpu.SMEM)
BF16 = jnp.bfloat16
F32 = jnp.float32
LIMIT = 24 * 1024 * 1024


def partner(index, step, size):
    return index ^ step if size & (size - 1) == 0 else (index + step) % size


def split(x):
    high = x.astype(BF16)
    return high, (x - high.astype(F32)).astype(BF16)


def cost(us):
    return pl.CostEstimate(flops=int(us * 1e9), bytes_accessed=1024, transcendentals=0)


def contract_last(a, b, **kw):
    return lax.dot_general(a, b, (((1,), (1,)), ((), ())), preferred_element_type=F32, **kw)


def inverse_scale(scale_ref):
    return jnp.sqrt(F32(5.0)) / scale_ref[...]


def fill_rows(block, inverse, x_ref, norm_ref, at, here):
    x = block * inverse
    norm = jnp.sum(x * x, axis=1, keepdims=True)
    high, low = split(-2.0 * x)
    features = x.shape[1]
    x_ref[pl.ds(at, here), :features] = high
    x_ref[pl.ds(at, here), features:] = low
    norm_ref[pl.ds(at, here), :] = jnp.broadcast_to(norm, (here, norm_ref.shape[1]))


def rows_kernel(n, scale_ref, *refs):
    blocks, (x_ref, norm_ref) = refs[:n], refs[n:]
    here = blocks[0].shape[0]
    inverse = inverse_scale(scale_ref)
    for i, block in enumerate(blocks):
        fill_rows(block[...], inverse, x_ref, norm_ref, i * here, here)


def prepare_rows(scale, blocks, us):
    here, features = blocks[0].shape
    m = here * len(blocks)
    return pl.pallas_call(
        functools.partial(rows_kernel, len(blocks)),
        out_shape=(jax.ShapeDtypeStruct((m, 2 * features), BF16), jax.ShapeDtypeStruct((m, 128), F32)),
        in_specs=[VMEM] * (1 + len(blocks)),
        out_specs=(VMEM, VMEM),
        compiler_params=pltpu.CompilerParams(vmem_limit_bytes=LIMIT),
        cost_estimate=cost(us),
        name="rows",
    )(scale, *blocks)


def fill_cols(block, inverse, y_ref, v_ref, norm_ref):
    features = inverse.shape[1]
    y = block[:, :features] * inverse
    high, low = split(y)
    for i, part in enumerate((high, high, low, low)):
        y_ref[:, i * features : (i + 1) * features] = part
    squares = y * y
    ones = jnp.ones((8, features), F32)
    norm_ref[...] = contract_last(ones, squares, precision=lax.Precision.HIGHEST)
    vhigh, vlow = split(block[:, features:])
    v_ref[:, : vhigh.shape[1]] = vhigh
    v_ref[:, vhigh.shape[1] :] = vlow


def times_tile(x, norm, y_ref, v_ref, col_norm_ref, amplitude):
    dist2 = contract_last(jnp.concatenate([x, x], axis=1), y_ref[...])
    dist2 = jnp.maximum(dist2 + norm[:, :1] + col_norm_ref[:1, :], 1e-30)
    a = dist2 * lax.rsqrt(dist2)
    tile = (amplitude + amplitude * a + (amplitude / 3.0) * dist2) * jnp.exp(-a)
    high, low = split(tile)
    columns = v_ref.shape[1] // 2
    out = jnp.dot(high, v_ref[...], preferred_element_type=F32)
    out = out[:, :columns] + out[:, columns:]
    return out + jnp.dot(low, v_ref[:, :columns], preferred_element_type=F32)


def tile_kernel(plan, here, scale_ref, amp_ref, *refs):
    n_parts, has_start = plan
    parts, refs = refs[:n_parts], refs[n_parts:]
    x_ref, norm_ref, refs = refs[0], refs[1], refs[2:]
    if has_start:
        start_ref, refs = refs[0], refs[1:]
    out_ref, y_ref, v_ref, col_norm_ref = refs
    inverse = inverse_scale(scale_ref)
    amplitude = amp_ref[0]
    for p, part in enumerate(parts):
        fill_cols(part[...], inverse, y_ref, v_ref, col_norm_ref)
        for i in range(x_ref.shape[0] // here):
            at = slice(i * here, (i + 1) * here)
            out = times_tile(x_ref[at, :], norm_ref[at, :], y_ref, v_ref, col_norm_ref, amplitude)
            if p > 0:
                out = out + out_ref[at, :]
            elif has_start:
                out = out + start_ref[at, :]
            out_ref[at, :] = out


def times_columns(scale, amplitude, parts, rows, start, here, us):
    x, norm = rows
    m = x.shape[0]
    n, width = parts[0].shape
    features = scale.shape[1]
    columns = width - features
    given = [scale, amplitude, *parts, x, norm] + ([] if start is None else [start])
    specs = [VMEM, SMEM] + [VMEM] * (len(given) - 2)
    return pl.pallas_call(
        functools.partial(tile_kernel, (len(parts), start is not None), here),
        out_shape=jax.ShapeDtypeStruct((m, columns), F32),
        in_specs=specs,
        out_specs=VMEM,
        scratch_shapes=[
            pltpu.VMEM((n, 4 * features), BF16),
            pltpu.VMEM((n, 2 * columns), BF16),
            pltpu.VMEM((8, n), F32),
        ],
        compiler_params=pltpu.CompilerParams(vmem_limit_bytes=LIMIT),
        cost_estimate=cost(us),
        name="tile",
    )(*given)


def solution(mesh):
    n_outer, n_inner = mesh.shape["outer"], mesh.shape["inner"]
    n_line = n_inner // CORES

    def linear(outer, line, core):
        return outer * n_inner + line * CORES + core

    places = [(o, z, c) for o in range(n_outer) for z in range(n_line) for c in range(CORES)]

    def along_line(step):
        return [(linear(o, z, c), linear(o, partner(z, step, n_line), c)) for o, z, c in places]

    def along_outer(step):
        return [(linear(o, z, c), linear(partner(o, step, n_outer), z, c)) for o, z, c in places]

    other_core = [(linear(o, z, c), linear(o, z, c ^ 1)) for o, z, c in places]

    def per_device(points, vectors, lengthscales, outputscale, noise):
        here = points.shape[0]
        scale = lengthscales[None, :]
        lines = list(range(n_line - 1, 0, -1))
        far_lines, near_line = lines[:-1], lines[-1]
        n_far = here * len(far_lines)
        far = [lax.ppermute(points, AXES, along_line(k)) for k in far_lines]
        both = jnp.concatenate([points, vectors], axis=1)
        got = [lax.ppermute(both, AXES, along_outer(k)) for k in range(n_outer - 1, 0, -1)]
        late = lax.optimization_barrier((points, *got))
        near = lax.ppermute(late[0], AXES, along_line(near_line))
        cols_mine = jnp.concatenate([both, *late[1:]], axis=0)
        cols_theirs = lax.ppermute(cols_mine, AXES, other_core)

        x, norm = prepare_rows(scale, [*far, points], 40)
        first = times_columns(scale, outputscale, [cols_mine], (x, norm), None, here, 20)
        partial = times_columns(
            scale, outputscale, [cols_theirs], (x[:n_far], norm[:n_far]), first[:n_far], here, 10
        )
        x_near, norm_near = prepare_rows(scale, [near], 1)
        partial_near = times_columns(scale, outputscale, [cols_mine, cols_theirs], (x_near, norm_near), None, here, 10)
        own = times_columns(
            scale, outputscale, [cols_theirs], (x[n_far:], norm[n_far:]), first[n_far:], here, 10
        )
        total = own + noise[0] * vectors
        for i, k in enumerate(lines):
            back = [(b, a) for a, b in along_line(k)]
            sent = partial[i * here : (i + 1) * here] if i < len(far_lines) else partial_near
            total = total + lax.ppermute(sent, AXES, back)
        return total

    placed = (P(AXES, None), P(AXES, None), P(), P(), P())
    return jax.shard_map(per_device, mesh=mesh, in_specs=placed, out_specs=P(AXES, None), check_vma=False)
```

```python
import functools
import math

import jax
import jax.numpy as jnp
from jax import lax
from jax.experimental import pallas as pl
from jax.experimental.pallas import tpu as pltpu
from jax.sharding import PartitionSpec as P

AXES = ("outer", "inner")
CORES = 2
VMEM = pl.BlockSpec(memory_space=pltpu.VMEM)
SMEM = pl.BlockSpec(memory_space=pltpu.SMEM)
BF16 = jnp.bfloat16
F32 = jnp.float32
LIMIT = 24 * 1024 * 1024
LANES = 128
LN2 = math.log(2.0)


def partner(index, step, size):
    return index ^ step if size & (size - 1) == 0 else (index + step) % size


def split(x):
    high = x.astype(BF16)
    return high, (x - high.astype(F32)).astype(BF16)


def cost(us):
    return pl.CostEstimate(flops=int(us * 1e9), bytes_accessed=1024, transcendentals=0)


def params():
    return pltpu.CompilerParams(vmem_limit_bytes=LIMIT)


def kernel_scale(scale_ref):
    return (math.sqrt(5.0) / LN2) / scale_ref[...]


def norm_lanes(norm, first):
    high, mid = split(norm)
    low = (norm - high.astype(F32) - mid.astype(F32)).astype(BF16)
    lane = lax.broadcasted_iota(jnp.int32, (norm.shape[0], LANES), 1)
    out = jnp.where((lane >= 3 - first) & (lane < 6 - first), 1.0, 0.0)
    for i, part in enumerate((high, mid, low)):
        out = jnp.where(lane == first + i, part.astype(F32), out)
    return out.astype(BF16)


def put(ref, at, parts):
    start = 0
    for part in parts:
        ref[at, start : start + part.shape[1]] = part
        start += part.shape[1]


def fill_rows(x_ref, at, block, scale):
    x = block * scale
    norm = jnp.sum(x * x, axis=1, keepdims=True)
    high, low = split(-2.0 * x)
    put(x_ref, at, (high, low, high, low, norm_lanes(norm, 0)))


def fill_cols(y_ref, v_ref, block, scale, amplitude):
    features = scale.shape[1]
    y = block[:, :features] * scale
    norm = jnp.sum(y * y, axis=1, keepdims=True)
    high, low = split(y)
    put(y_ref, slice(None), (high, high, low, low, norm_lanes(norm, 3)))
    put(v_ref, slice(None), split(block[:, features:] * (amplitude * LN2)))


def rows_kernel(places, scale_ref, *refs):
    x_ref = refs[-1]
    scale = kernel_scale(scale_ref)
    for place, block in zip(places, refs):
        here = block.shape[0]
        fill_rows(x_ref, pl.ds(place * here, here), block[...], scale)


def prepare_rows(scale, blocks, places, total, x, us):
    here, features = blocks[0].shape
    given = [scale, *blocks] + ([] if x is None else [x])
    return pl.pallas_call(
        functools.partial(rows_kernel, places),
        out_shape=jax.ShapeDtypeStruct((here * total, 4 * features + LANES), BF16),
        in_specs=[VMEM] * len(given),
        out_specs=VMEM,
        input_output_aliases={} if x is None else {len(given) - 1: 0},
        compiler_params=params(),
        cost_estimate=cost(us),
        name="rows",
    )(*given)


def times_tile(x_ref, first, count, y_ref, v_ref):
    columns = v_ref.shape[1] // 2
    n = y_ref.shape[0]
    x = x_ref[first : first + count, :]
    total = None
    for at in range(0, n, 256):
        cols = slice(at, min(at + 256, n))
        b2 = lax.dot_general(x, y_ref[cols, :], (((1,), (1,)), ((), ())), preferred_element_type=F32)
        b2 = jnp.maximum(b2, 1e-30)
        b = b2 * lax.rsqrt(b2)
        tile = (b2 * (LN2 / 3.0) + b + (1.0 / LN2)) * jnp.exp2(-b)
        high, low = split(tile)
        part = jnp.dot(high, v_ref[cols, :], preferred_element_type=F32)
        part = part[:, :columns] + part[:, columns:]
        part = part + jnp.dot(low, v_ref[cols, :columns], preferred_element_type=F32)
        total = part if total is None else total + part
    return total


def tile_kernel(first, here, sizes, has_start, scale_ref, amp_ref, cols_ref, x_ref, *refs):
    n_in = 1 if has_start else 0
    given, outs, (y_ref, v_ref) = refs[:n_in], refs[n_in:-2], refs[-2:]
    fill_cols(y_ref, v_ref, cols_ref[...], kernel_scale(scale_ref), amp_ref[0])
    count = sum(sizes) * here
    total = times_tile(x_ref, first * here, count, y_ref, v_ref)
    if has_start:
        total = total + given[0][first * here : first * here + count, :]
    at = 0
    for size, out in zip(sizes, outs):
        out[...] = total[at * here : (at + size) * here, :]
        at += size


def times_columns(scale, amplitude, cols, x, first, sizes, start, here, us):
    n, width = cols.shape
    features = scale.shape[1]
    columns = width - features
    given = [scale, amplitude, cols, x] + ([] if start is None else [start])
    return pl.pallas_call(
        functools.partial(tile_kernel, first, here, sizes, start is not None),
        out_shape=[jax.ShapeDtypeStruct((size * here, columns), F32) for size in sizes],
        in_specs=[VMEM, SMEM] + [VMEM] * (len(given) - 2),
        out_specs=[VMEM] * len(sizes),
        scratch_shapes=[
            pltpu.VMEM((n, 4 * features + LANES), BF16),
            pltpu.VMEM((n, 2 * columns), BF16),
        ],
        compiler_params=params(),
        cost_estimate=cost(us),
        name="tile",
    )(*given)


def solution(mesh):
    n_outer, n_inner = mesh.shape["outer"], mesh.shape["inner"]
    n_line = n_inner // CORES

    def linear(outer, line, core):
        return outer * n_inner + line * CORES + core

    places = [(o, z, c) for o in range(n_outer) for z in range(n_line) for c in range(CORES)]

    def along_line(step):
        return [(linear(o, z, c), linear(o, partner(z, step, n_line), c)) for o, z, c in places]

    def along_outer(step):
        return [(linear(o, z, c), linear(partner(o, step, n_outer), z, c)) for o, z, c in places]

    other_core = [(linear(o, z, c), linear(o, z, c ^ 1)) for o, z, c in places]

    def per_device(points, vectors, lengthscales, outputscale, noise):
        here = points.shape[0]
        scale = lengthscales[None, :]
        lines = list(range(n_line - 1, 0, -1))
        far_lines, near_line = lines[:-1], lines[-1]
        n_far = len(far_lines)
        far = [lax.ppermute(points, AXES, along_line(k)) for k in far_lines]
        both = jnp.concatenate([points, vectors], axis=1)
        got = [lax.ppermute(both, AXES, along_outer(k)) for k in range(n_outer - 1, 0, -1)]
        late = lax.optimization_barrier((points, far[0]))
        near = lax.ppermute(late[0], AXES, along_line(near_line))
        cols_mine = jnp.concatenate([both, *got], axis=0)
        cols_theirs = lax.ppermute(cols_mine, AXES, other_core)

        x = prepare_rows(scale, [late[1], points], [0, n_far], n_line, None, 40)
        x = prepare_rows(scale, [*far[1:], near], [*range(1, n_far), n_line - 1], n_line, x, 1)
        tile = functools.partial(times_columns, scale, outputscale)
        (mine,) = tile(cols_mine, x, 0, [n_line], None, here, 20)
        back_far = tile(cols_theirs, x, 0, [1] * n_far, mine, here, 10)
        own, back_near = tile(cols_theirs, x, n_far, [1, 1], mine, here, 10)
        total = own + noise[0] * vectors
        for k, sent in zip(lines, [*back_far, back_near]):
            total = total + lax.ppermute(sent, AXES, [(b, a) for a, b in along_line(k)])
        return total

    placed = (P(AXES, None), P(AXES, None), P(), P(), P())
    return jax.shard_map(per_device, mesh=mesh, in_specs=placed, out_specs=P(AXES, None), check_vma=False)
```

```python
import functools
import math

import jax
import jax.numpy as jnp
from jax import lax
from jax.experimental import pallas as pl
from jax.experimental.pallas import tpu as pltpu
from jax.sharding import PartitionSpec as P

AXES = ("outer", "inner")
CORES = 2
VMEM = pl.BlockSpec(memory_space=pltpu.VMEM)
SMEM = pl.BlockSpec(memory_space=pltpu.SMEM)
BF16 = jnp.bfloat16
F32 = jnp.float32
LIMIT = 24 * 1024 * 1024
LANES = 128
LN2 = math.log(2.0)
GROUP = 4


def partner(index, step, size):
    return index ^ step if size & (size - 1) == 0 else (index + step) % size


def split(x):
    high = x.astype(BF16)
    return high, (x - high.astype(F32)).astype(BF16)


def cost(us):
    return pl.CostEstimate(flops=int(us * 1e9), bytes_accessed=1024, transcendentals=0)


def params():
    return pltpu.CompilerParams(vmem_limit_bytes=LIMIT)


def kernel_scale(scale_ref):
    return (math.sqrt(5.0) / LN2) / scale_ref[...]


def norm_lanes(norm, first):
    high, mid = split(norm)
    low = (norm - high.astype(F32) - mid.astype(F32)).astype(BF16)
    lane = lax.broadcasted_iota(jnp.int32, (norm.shape[0], LANES), 1)
    out = jnp.where((lane >= 3 - first) & (lane < 6 - first), 1.0, 0.0)
    for i, part in enumerate((high, mid, low)):
        out = jnp.where(lane == first + i, part.astype(F32), out)
    return out.astype(BF16)


def put(ref, at, parts):
    start = 0
    for part in parts:
        ref[at, start : start + part.shape[1]] = part
        start += part.shape[1]


def fill_rows(x_ref, at, block, scale):
    x = block * scale
    norm = jnp.sum(x * x, axis=1, keepdims=True)
    high, low = split(-2.0 * x)
    put(x_ref, at, (high, low, high, low, norm_lanes(norm, 0)))


def fill_cols(y_ref, v_ref, block, scale, amplitude):
    features = scale.shape[1]
    y = block[:, :features] * scale
    norm = jnp.sum(y * y, axis=1, keepdims=True)
    high, low = split(y)
    put(y_ref, slice(None), (high, high, low, low, norm_lanes(norm, 3)))
    put(v_ref, slice(None), split(block[:, features:] * (amplitude * LN2)))


def rows_kernel(places, scale_ref, *refs):
    x_ref = refs[-1]
    scale = kernel_scale(scale_ref)
    for place, block in zip(places, refs):
        here = block.shape[0]
        fill_rows(x_ref, pl.ds(place * here, here), block[...], scale)


def prepare_rows(scale, blocks, places, total, x, us):
    here, features = blocks[0].shape
    given = [scale, *blocks] + ([] if x is None else [x])
    return pl.pallas_call(
        functools.partial(rows_kernel, places),
        out_shape=jax.ShapeDtypeStruct((here * total, 4 * features + LANES), BF16),
        in_specs=[VMEM] * len(given),
        out_specs=VMEM,
        input_output_aliases={} if x is None else {len(given) - 1: 0},
        compiler_params=params(),
        cost_estimate=cost(us),
        name="rows",
    )(*given)


def times_tile(x, y_ref, v_ref):
    columns = v_ref.shape[1] // 2
    b2 = lax.dot_general(x, y_ref[...], (((1,), (1,)), ((), ())), preferred_element_type=F32)
    b2 = jnp.maximum(b2, 1e-30)
    b = b2 * lax.rsqrt(b2)
    high, low = split((b2 * (LN2 / 3.0) + b + (1.0 / LN2)) * jnp.exp2(-b))
    total = jnp.dot(high, v_ref[...], preferred_element_type=F32)
    return total[:, :columns] + total[:, columns:] + jnp.dot(low, v_ref[:, :columns], preferred_element_type=F32)


def tile_kernel(first, here, sizes, has_start, scale_ref, amp_ref, cols_ref, x_ref, *refs):
    n_in = 1 if has_start else 0
    given, outs, (y_ref, v_ref) = refs[:n_in], refs[n_in:-2], refs[-2:]
    fill_cols(y_ref, v_ref, cols_ref[...], kernel_scale(scale_ref), amp_ref[0])
    blocks = [(out, i) for out, size in zip(outs, sizes) for i in range(size)]
    for at in range(0, len(blocks), GROUP):
        group = blocks[at : at + GROUP]
        rows = slice((first + at) * here, (first + at + len(group)) * here)
        total = times_tile(x_ref[rows, :], y_ref, v_ref)
        if has_start:
            total = total + given[0][rows, :]
        for j, (out, i) in enumerate(group):
            out[i * here : (i + 1) * here, :] = total[j * here : (j + 1) * here, :]


def times_columns(scale, amplitude, cols, x, first, sizes, start, here, us):
    n, width = cols.shape
    features = scale.shape[1]
    columns = width - features
    given = [scale, amplitude, cols, x] + ([] if start is None else [start])
    return pl.pallas_call(
        functools.partial(tile_kernel, first, here, sizes, start is not None),
        out_shape=[jax.ShapeDtypeStruct((size * here, columns), F32) for size in sizes],
        in_specs=[VMEM, SMEM] + [VMEM] * (len(given) - 2),
        out_specs=[VMEM] * len(sizes),
        scratch_shapes=[
            pltpu.VMEM((n, 4 * features + LANES), BF16),
            pltpu.VMEM((n, 2 * columns), BF16),
        ],
        compiler_params=params(),
        cost_estimate=cost(us),
        name="tile",
    )(*given)


def solution(mesh):
    n_outer, n_inner = mesh.shape["outer"], mesh.shape["inner"]
    n_line = n_inner // CORES

    def linear(outer, line, core):
        return outer * n_inner + line * CORES + core

    places = [(o, z, c) for o in range(n_outer) for z in range(n_line) for c in range(CORES)]

    def along_line(step):
        return [(linear(o, z, c), linear(o, partner(z, step, n_line), c)) for o, z, c in places]

    def along_outer(step):
        return [(linear(o, z, c), linear(partner(o, step, n_outer), z, c)) for o, z, c in places]

    other_core = [(linear(o, z, c), linear(o, z, c ^ 1)) for o, z, c in places]

    def per_device(points, vectors, lengthscales, outputscale, noise):
        here = points.shape[0]
        scale = lengthscales[None, :]
        lines = list(range(n_line - 1, 0, -1))
        far_lines, near_line = lines[:-1], lines[-1]
        n_far = len(far_lines)
        far = [lax.ppermute(points, AXES, along_line(k)) for k in far_lines]
        both = jnp.concatenate([points, vectors], axis=1)
        got = [lax.ppermute(both, AXES, along_outer(k)) for k in range(n_outer - 1, 0, -1)]
        late = lax.optimization_barrier((points, far[0]))
        near = lax.ppermute(late[0], AXES, along_line(near_line))
        cols_mine = jnp.concatenate([both, *got], axis=0)
        cols_theirs = lax.ppermute(cols_mine, AXES, other_core)

        x = prepare_rows(scale, [late[1], points], [0, n_far], n_line, None, 40)
        x = prepare_rows(scale, [*far[1:], near], [*range(1, n_far), n_line - 1], n_line, x, 1)
        tile = functools.partial(times_columns, scale, outputscale)
        (mine,) = tile(cols_mine, x, 0, [n_line], None, here, 20)
        back_far = tile(cols_theirs, x, 0, [1] * n_far, mine, here, 10)
        own, back_near = tile(cols_theirs, x, n_far, [1, 1], mine, here, 10)
        total = own + noise[0] * vectors
        for k, sent in zip(lines, [*back_far, back_near]):
            total = total + lax.ppermute(sent, AXES, [(b, a) for a, b in along_line(k)])
        return total

    placed = (P(AXES, None), P(AXES, None), P(), P(), P())
    return jax.shard_map(per_device, mesh=mesh, in_specs=placed, out_specs=P(AXES, None), check_vma=False)
```

```python
import functools
import math

import jax
import jax.numpy as jnp
from jax import lax
from jax.experimental import pallas as pl
from jax.experimental.pallas import tpu as pltpu
from jax.sharding import PartitionSpec as P

AXES = ("outer", "inner")
CORES = 2
VMEM = pl.BlockSpec(memory_space=pltpu.VMEM)
SMEM = pl.BlockSpec(memory_space=pltpu.SMEM)
BF16 = jnp.bfloat16
F32 = jnp.float32
LIMIT = 24 * 1024 * 1024
LANES = 128
LN2 = math.log(2.0)
GROUP = 4


def partner(index, step, size):
    return index ^ step if size & (size - 1) == 0 else (index + step) % size


def split(x):
    high = x.astype(BF16)
    return high, (x - high.astype(F32)).astype(BF16)


def cost(us):
    return pl.CostEstimate(flops=int(us * 1e9), bytes_accessed=1024, transcendentals=0)


def params():
    return pltpu.CompilerParams(vmem_limit_bytes=LIMIT)


def kernel_scale(scale_ref):
    return (math.sqrt(5.0) / LN2) / scale_ref[...]


def norm_lanes(norm, first):
    high, mid = split(norm)
    low = (norm - high.astype(F32) - mid.astype(F32)).astype(BF16)
    lane = lax.broadcasted_iota(jnp.int32, (norm.shape[0], LANES), 1)
    out = jnp.where((lane >= 3 - first) & (lane < 6 - first), 1.0, 0.0)
    for i, part in enumerate((high, mid, low)):
        out = jnp.where(lane == first + i, part.astype(F32), out)
    return out.astype(BF16)


def put(ref, at, parts):
    start = 0
    for part in parts:
        ref[at, start : start + part.shape[1]] = part
        start += part.shape[1]


def fill_rows(x_ref, at, block, scale):
    x = block * scale
    norm = jnp.sum(x * x, axis=1, keepdims=True)
    high, low = split(-2.0 * x)
    put(x_ref, at, (high, low, high, low, norm_lanes(norm, 0)))


def fill_cols(y_ref, v_ref, at, block, scale, amplitude):
    features = scale.shape[1]
    y = block[:, :features] * scale
    norm = jnp.sum(y * y, axis=1, keepdims=True)
    high, low = split(y)
    put(y_ref, at, (high, high, low, low, norm_lanes(norm, 3)))
    put(v_ref, at, split(block[:, features:] * (amplitude * LN2)))


def blank_kernel(out_ref):
    out_ref[...] = jnp.zeros_like(out_ref)


def blank(shape, us):
    return pl.pallas_call(
        blank_kernel,
        out_shape=jax.ShapeDtypeStruct(shape, F32),
        out_specs=VMEM,
        compiler_params=params(),
        cost_estimate=cost(us),
        name="blank",
    )()


def join_kernel(a_ref, b_ref, _, out_ref):
    put(out_ref, slice(None), (a_ref[...], b_ref[...]))


def join(a, b, out):
    return pl.pallas_call(
        join_kernel,
        out_shape=jax.ShapeDtypeStruct(out.shape, out.dtype),
        in_specs=[VMEM] * 3,
        out_specs=VMEM,
        input_output_aliases={2: 0},
        compiler_params=params(),
        cost_estimate=cost(1),
        name="join",
    )(a, b, out)


def rows_kernel(scale_ref, *refs):
    n = len(refs) // 2
    scale = kernel_scale(scale_ref)
    for block, x_ref in zip(refs[:n], refs[n:]):
        fill_rows(x_ref, slice(None), block[...], scale)


def prepare_rows(scale, blocks, us):
    here, features = blocks[0].shape
    return pl.pallas_call(
        rows_kernel,
        out_shape=[jax.ShapeDtypeStruct((here, 4 * features + LANES), BF16)] * len(blocks),
        in_specs=[VMEM] * (1 + len(blocks)),
        out_specs=[VMEM] * len(blocks),
        compiler_params=params(),
        cost_estimate=cost(us),
        name="rows",
    )(scale, *blocks)


def times_tile(x, y_ref, v_ref):
    columns = v_ref.shape[1] // 2
    b2 = lax.dot_general(x, y_ref[...], (((1,), (1,)), ((), ())), preferred_element_type=F32)
    b2 = jnp.maximum(b2, 1e-30)
    b = b2 * lax.rsqrt(b2)
    high, low = split((b2 * (LN2 / 3.0) + b + (1.0 / LN2)) * jnp.exp2(-b))
    total = jnp.dot(high, v_ref[...], preferred_element_type=F32)
    return total[:, :columns] + total[:, columns:] + jnp.dot(low, v_ref[:, :columns], preferred_element_type=F32)


def fill_all(cols, y_ref, v_ref, scale, amplitude):
    at = 0
    for block in cols:
        fill_cols(y_ref, v_ref, slice(at, at + block.shape[0]), block[...], scale, amplitude)
        at += block.shape[0]


def groups(n):
    return [range(first, min(first + GROUP, n)) for first in range(0, n, GROUP)]


def tile_kernel(n_cols, n_rows, scale_ref, amp_ref, noise_ref, *refs):
    cols, rows, rest = refs[:n_cols], refs[n_cols : n_cols + n_rows], refs[n_cols + n_rows :]
    starts, outs, (y_ref, v_ref) = rest[: -n_rows - 2], rest[-n_rows - 2 : -2], rest[-2:]
    here = rows[0].shape[0]
    fill_all(cols, y_ref, v_ref, kernel_scale(scale_ref), amp_ref[0])
    for group in groups(n_rows):
        total = times_tile(jnp.concatenate([rows[i][...] for i in group], axis=0), y_ref, v_ref)
        for j, i in enumerate(group):
            out = total[j * here : (j + 1) * here, :]
            if starts:
                out = out + starts[i][...]
            elif i == 0:
                out = out + noise_ref[0] * cols[0][:here, -out.shape[1] :]
            outs[i][...] = out


def prepared_shapes(cols, features):
    n, width = sum(block.shape[0] for block in cols), cols[0].shape[1]
    return [
        jax.ShapeDtypeStruct((n, 4 * features + LANES), BF16),
        jax.ShapeDtypeStruct((n, 2 * (width - features)), BF16),
    ]


def times_columns(scale, amplitude, noise, cols, rows, starts, us):
    here = rows[0].shape[0]
    features = scale.shape[1]
    given = [scale, amplitude, noise, *cols, *rows, *starts]
    *outs, y, v = pl.pallas_call(
        functools.partial(tile_kernel, len(cols), len(rows)),
        out_shape=[jax.ShapeDtypeStruct((here, cols[0].shape[1] - features), F32)] * len(rows)
        + prepared_shapes(cols, features),
        in_specs=[VMEM, SMEM, SMEM] + [VMEM] * (len(given) - 3),
        out_specs=[VMEM] * (len(rows) + 2),
        compiler_params=params(),
        cost_estimate=cost(us),
        name="tile",
    )(*given)
    return outs, (y, v)


def last_kernel(n_blocks, scale_ref, *refs):
    blocks, prepared, outs, xs = refs[:n_blocks], refs[n_blocks : -2 * n_blocks], refs[-2 * n_blocks : -n_blocks], refs[-n_blocks:]
    scale = kernel_scale(scale_ref)
    here = blocks[0].shape[0]
    for block, x_ref in zip(blocks, xs):
        fill_rows(x_ref, slice(None), block[...], scale)
    for group in groups(n_blocks):
        x = jnp.concatenate([xs[i][...] for i in group], axis=0)
        total = times_tile(x, *prepared)
        for j, i in enumerate(group):
            outs[i][...] = total[j * here : (j + 1) * here, :]


def times_prepared(scale, blocks, prepared, us):
    n = len(blocks)
    here, features = blocks[0].shape
    columns = prepared[0][1].shape[1] // 2
    given = [scale, *blocks, *prepared[0]]
    out = pl.pallas_call(
        functools.partial(last_kernel, n),
        out_shape=[jax.ShapeDtypeStruct((here, columns), F32)] * n
        + [jax.ShapeDtypeStruct((here, 4 * features + LANES), BF16)] * n,
        in_specs=[VMEM] * len(given),
        out_specs=[VMEM] * (2 * n),
        compiler_params=params(),
        cost_estimate=cost(us),
        name="last",
    )(*given)
    return out[:n], out[n:]


def near_kernel(y_ref, v_ref, *refs):
    n = len(refs) // 3
    rows, starts, outs = refs[:n], refs[n : 2 * n], refs[2 * n :]
    here = rows[0].shape[0]
    total = times_tile(jnp.concatenate([row[...] for row in rows], axis=0), y_ref, v_ref)
    for i in range(n):
        outs[i][...] = starts[i][...] + total[i * here : (i + 1) * here, :]


def times_near(prepared, rows, starts, us):
    return pl.pallas_call(
        near_kernel,
        out_shape=[jax.ShapeDtypeStruct(start.shape, F32) for start in starts],
        in_specs=[VMEM] * (2 + 2 * len(rows)),
        out_specs=[VMEM] * len(rows),
        compiler_params=params(),
        cost_estimate=cost(us),
        name="near",
    )(*prepared, *rows, *starts)


def add_kernel(*refs):
    out = refs[0][...]
    for ref in refs[1:-1]:
        out = out + ref[...]
    refs[-1][...] = out


def add_most(parts, us):
    return pl.pallas_call(
        add_kernel,
        out_shape=jax.ShapeDtypeStruct(parts[0].shape, F32),
        in_specs=[VMEM] * len(parts),
        out_specs=VMEM,
        compiler_params=params(),
        cost_estimate=cost(us),
        name="add",
    )(*parts)


def solution(mesh):
    n_outer, n_inner = mesh.shape["outer"], mesh.shape["inner"]
    n_line = n_inner // CORES

    def linear(outer, line, core):
        return outer * n_inner + line * CORES + core

    places = [(o, z, c) for o in range(n_outer) for z in range(n_line) for c in range(CORES)]

    def along_line(step):
        return [(linear(o, z, c), linear(o, partner(z, step, n_line), c)) for o, z, c in places]

    def along_outer(step):
        return [(linear(o, z, c), linear(partner(o, step, n_outer), z, c)) for o, z, c in places]

    other_core = [(linear(o, z, c), linear(o, z, c ^ 1)) for o, z, c in places]

    def per_device(points, vectors, lengthscales, outputscale, noise):
        scale = lengthscales[None, :]
        half = n_line // 2
        direct = list(range(1, half + 1))
        forwarded = list(range(half + 1, n_line))
        points_of = {half: lax.ppermute(points, AXES, along_line(half))}
        here, features = points.shape
        both = blank((here, features + vectors.shape[1]), 20)
        both = join(points, vectors, both)
        got = [lax.ppermute(both, AXES, along_outer(k)) for k in range(n_outer - 1, 0, -1)]
        for k in direct[:-1]:
            points_of[k] = lax.ppermute(points, AXES, along_line(k))
        for k in forwarded:
            points_of[k] = lax.ppermute(points_of[half], AXES, along_line(k - half))
        cols_mine = jnp.concatenate([both, *got], axis=0)
        cols_theirs = lax.ppermute(cols_mine, AXES, other_core)

        x = dict(zip([half, 0], prepare_rows(scale, [points_of[half], points], 40)))
        x |= dict(zip(direct[:-1], prepare_rows(scale, [points_of[k] for k in direct[:-1]], 1)))
        ks = [0, *direct]
        part, mine = times_columns(scale, outputscale, noise, [cols_mine], [x[k] for k in ks], [], 20)
        total = dict(zip(ks, part))
        last = lax.optimization_barrier((*[points_of[k] for k in forwarded], *part))[: len(forwarded)]
        part, x_last = times_prepared(scale, last, [mine], 10)
        total |= dict(zip(forwarded, part))
        x |= dict(zip(forwarded, x_last))
        ks = [*forwarded, *direct[1:]]
        part, theirs = times_columns(scale, outputscale, noise, [cols_theirs], [x[k] for k in ks], [total[k] for k in ks], 10)
        total |= dict(zip(ks, part))
        total |= dict(zip([0, 1], times_near(theirs, [x[0], x[1]], [total[0], total[1]], 10)))
        got = [
            lax.ppermute(total[k], AXES, [(b, a) for a, b in along_line(k)]) for k in [*direct[1:], *forwarded, 1]
        ]
        return add_most([total[0], *got[:-1]], 10) + got[-1]

    placed = (P(AXES, None), P(AXES, None), P(), P(), P())
    return jax.shard_map(per_device, mesh=mesh, in_specs=placed, out_specs=P(AXES, None), check_vma=False)
```

```python
import functools
import math

import jax
import jax.numpy as jnp
from jax import lax
from jax.experimental import pallas as pl
from jax.experimental.pallas import tpu as pltpu
from jax.sharding import PartitionSpec as P

AXES = ("outer", "inner")
CORES = 2
VMEM = pl.BlockSpec(memory_space=pltpu.VMEM)
SMEM = pl.BlockSpec(memory_space=pltpu.SMEM)
BF16 = jnp.bfloat16
F32 = jnp.float32
LIMIT = 24 * 1024 * 1024
LANES = 128
LN2 = math.log(2.0)
GROUP = 4


def partner(index, step, size):
    return index ^ step if size & (size - 1) == 0 else (index + step) % size


def split(x):
    high = x.astype(BF16)
    return high, (x - high.astype(F32)).astype(BF16)


def cost(us):
    return pl.CostEstimate(flops=int(us * 1e9), bytes_accessed=1024, transcendentals=0)


def params():
    return pltpu.CompilerParams(vmem_limit_bytes=LIMIT)


def kernel_scale(scale_ref):
    return (math.sqrt(5.0) / LN2) / scale_ref[...]


def norm_lanes(norm, first):
    high, mid = split(norm)
    low = (norm - high.astype(F32) - mid.astype(F32)).astype(BF16)
    lane = lax.broadcasted_iota(jnp.int32, (norm.shape[0], LANES), 1)
    out = jnp.where((lane >= 3 - first) & (lane < 6 - first), 1.0, 0.0)
    for i, part in enumerate((high, mid, low)):
        out = jnp.where(lane == first + i, part.astype(F32), out)
    return out.astype(BF16)


def put(ref, at, parts):
    start = 0
    for part in parts:
        ref[at, start : start + part.shape[1]] = part
        start += part.shape[1]


def fill_rows(x_ref, at, block, scale):
    high, low = split(block * scale)
    x = high.astype(F32) + low.astype(F32)
    norm = jnp.sum(x * x, axis=1, keepdims=True)
    high, low = (-2.0 * high.astype(F32)).astype(BF16), (-2.0 * low.astype(F32)).astype(BF16)
    put(x_ref, at, (high, low, high, low, norm_lanes(norm, 0)))


def fill_cols(y_ref, v_ref, at, block, scale, amplitude):
    features = scale.shape[1]
    high, low = split(block[:, :features] * scale)
    y = high.astype(F32) + low.astype(F32)
    norm = jnp.sum(y * y, axis=1, keepdims=True)
    put(y_ref, at, (high, high, low, low, norm_lanes(norm, 3)))
    put(v_ref, at, split(block[:, features:] * (amplitude * LN2)))


def blank_kernel(out_ref):
    out_ref[...] = jnp.zeros_like(out_ref)


def blank(shape, us):
    return pl.pallas_call(
        blank_kernel,
        out_shape=jax.ShapeDtypeStruct(shape, F32),
        out_specs=VMEM,
        compiler_params=params(),
        cost_estimate=cost(us),
        name="blank",
    )()


def join_kernel(a_ref, b_ref, _, out_ref):
    put(out_ref, slice(None), (a_ref[...], b_ref[...]))


def join(a, b, out):
    return pl.pallas_call(
        join_kernel,
        out_shape=jax.ShapeDtypeStruct(out.shape, out.dtype),
        in_specs=[VMEM] * 3,
        out_specs=VMEM,
        input_output_aliases={2: 0},
        compiler_params=params(),
        cost_estimate=cost(1),
        name="join",
    )(a, b, out)


def rows_kernel(scale_ref, *refs):
    n = len(refs) // 2
    scale = kernel_scale(scale_ref)
    for block, x_ref in zip(refs[:n], refs[n:]):
        fill_rows(x_ref, slice(None), block[...], scale)


def prepare_rows(scale, blocks, us):
    here, features = blocks[0].shape
    return pl.pallas_call(
        rows_kernel,
        out_shape=[jax.ShapeDtypeStruct((here, 4 * features + LANES), BF16)] * len(blocks),
        in_specs=[VMEM] * (1 + len(blocks)),
        out_specs=[VMEM] * len(blocks),
        compiler_params=params(),
        cost_estimate=cost(us),
        name="rows",
    )(scale, *blocks)


def times_tile(x, y_ref, v_ref):
    columns = v_ref.shape[1] // 2
    b2 = lax.dot_general(x, y_ref[...], (((1,), (1,)), ((), ())), preferred_element_type=F32)
    b2 = jnp.maximum(b2, 1e-30)
    b = b2 * lax.rsqrt(b2)
    high, low = split((b2 * (LN2 / 3.0) + b + (1.0 / LN2)) * jnp.exp2(-b))
    total = jnp.dot(high, v_ref[...], preferred_element_type=F32)
    return total[:, :columns] + total[:, columns:] + jnp.dot(low, v_ref[:, :columns], preferred_element_type=F32)


def fill_all(cols, y_ref, v_ref, scale, amplitude):
    at = 0
    for block in cols:
        fill_cols(y_ref, v_ref, slice(at, at + block.shape[0]), block[...], scale, amplitude)
        at += block.shape[0]


def groups(n):
    return [range(first, min(first + GROUP, n)) for first in range(0, n, GROUP)]


def tile_kernel(n_cols, n_rows, scale_ref, amp_ref, noise_ref, *refs):
    cols, rows, rest = refs[:n_cols], refs[n_cols : n_cols + n_rows], refs[n_cols + n_rows :]
    starts, outs, (y_ref, v_ref) = rest[: -n_rows - 2], rest[-n_rows - 2 : -2], rest[-2:]
    here = rows[0].shape[0]
    fill_all(cols, y_ref, v_ref, kernel_scale(scale_ref), amp_ref[0])
    for group in groups(n_rows):
        total = times_tile(jnp.concatenate([rows[i][...] for i in group], axis=0), y_ref, v_ref)
        for j, i in enumerate(group):
            out = total[j * here : (j + 1) * here, :]
            if starts:
                out = out + starts[i][...]
            elif i == 0:
                out = out + noise_ref[0] * cols[0][:here, -out.shape[1] :]
            outs[i][...] = out


def prepared_shapes(cols, features):
    n, width = sum(block.shape[0] for block in cols), cols[0].shape[1]
    return [
        jax.ShapeDtypeStruct((n, 4 * features + LANES), BF16),
        jax.ShapeDtypeStruct((n, 2 * (width - features)), BF16),
    ]


def times_columns(scale, amplitude, noise, cols, rows, starts, us):
    here = rows[0].shape[0]
    features = scale.shape[1]
    given = [scale, amplitude, noise, *cols, *rows, *starts]
    *outs, y, v = pl.pallas_call(
        functools.partial(tile_kernel, len(cols), len(rows)),
        out_shape=[jax.ShapeDtypeStruct((here, cols[0].shape[1] - features), F32)] * len(rows)
        + prepared_shapes(cols, features),
        in_specs=[VMEM, SMEM, SMEM] + [VMEM] * (len(given) - 3),
        out_specs=[VMEM] * (len(rows) + 2),
        compiler_params=params(),
        cost_estimate=cost(us),
        name="tile",
    )(*given)
    return outs, (y, v)


def last_kernel(n_blocks, scale_ref, *refs):
    blocks, prepared, outs, xs = refs[:n_blocks], refs[n_blocks : -2 * n_blocks], refs[-2 * n_blocks : -n_blocks], refs[-n_blocks:]
    scale = kernel_scale(scale_ref)
    here = blocks[0].shape[0]
    for block, x_ref in zip(blocks, xs):
        fill_rows(x_ref, slice(None), block[...], scale)
    for group in groups(n_blocks):
        x = jnp.concatenate([xs[i][...] for i in group], axis=0)
        total = times_tile(x, *prepared)
        for j, i in enumerate(group):
            outs[i][...] = total[j * here : (j + 1) * here, :]


def times_prepared(scale, blocks, prepared, us):
    n = len(blocks)
    here, features = blocks[0].shape
    columns = prepared[0][1].shape[1] // 2
    given = [scale, *blocks, *prepared[0]]
    out = pl.pallas_call(
        functools.partial(last_kernel, n),
        out_shape=[jax.ShapeDtypeStruct((here, columns), F32)] * n
        + [jax.ShapeDtypeStruct((here, 4 * features + LANES), BF16)] * n,
        in_specs=[VMEM] * len(given),
        out_specs=[VMEM] * (2 * n),
        compiler_params=params(),
        cost_estimate=cost(us),
        name="last",
    )(*given)
    return out[:n], out[n:]


def near_kernel(y_ref, v_ref, *refs):
    n = len(refs) // 3
    rows, starts, outs = refs[:n], refs[n : 2 * n], refs[2 * n :]
    here = rows[0].shape[0]
    total = times_tile(jnp.concatenate([row[...] for row in rows], axis=0), y_ref, v_ref)
    for i in range(n):
        outs[i][...] = starts[i][...] + total[i * here : (i + 1) * here, :]


def times_near(prepared, rows, starts, us):
    return pl.pallas_call(
        near_kernel,
        out_shape=[jax.ShapeDtypeStruct(start.shape, F32) for start in starts],
        in_specs=[VMEM] * (2 + 2 * len(rows)),
        out_specs=[VMEM] * len(rows),
        compiler_params=params(),
        cost_estimate=cost(us),
        name="near",
    )(*prepared, *rows, *starts)


def add_kernel(*refs):
    out = refs[0][...]
    for ref in refs[1:-1]:
        out = out + ref[...]
    refs[-1][...] = out


def add_most(parts, us):
    return pl.pallas_call(
        add_kernel,
        out_shape=jax.ShapeDtypeStruct(parts[0].shape, F32),
        in_specs=[VMEM] * len(parts),
        out_specs=VMEM,
        compiler_params=params(),
        cost_estimate=cost(us),
        name="add",
    )(*parts)


def solution(mesh):
    n_outer, n_inner = mesh.shape["outer"], mesh.shape["inner"]
    n_line = n_inner // CORES

    def linear(outer, line, core):
        return outer * n_inner + line * CORES + core

    places = [(o, z, c) for o in range(n_outer) for z in range(n_line) for c in range(CORES)]

    def along_line(step):
        return [(linear(o, z, c), linear(o, partner(z, step, n_line), c)) for o, z, c in places]

    def along_outer(step):
        return [(linear(o, z, c), linear(partner(o, step, n_outer), z, c)) for o, z, c in places]

    other_core = [(linear(o, z, c), linear(o, z, c ^ 1)) for o, z, c in places]

    def per_device(points, vectors, lengthscales, outputscale, noise):
        scale = lengthscales[None, :]
        half = n_line // 2
        direct = list(range(1, half + 1))
        forwarded = list(range(half + 1, n_line))
        points_of = {half: lax.ppermute(points, AXES, along_line(half))}
        here, features = points.shape
        both = blank((here, features + vectors.shape[1]), 20)
        both = join(points, vectors, both)
        got = [lax.ppermute(both, AXES, along_outer(k)) for k in [n_outer - 1, *range(1, n_outer - 1)]]
        for k in direct[:-1]:
            points_of[k] = lax.ppermute(points, AXES, along_line(k))
        for k in forwarded:
            points_of[k] = lax.ppermute(points_of[half], AXES, along_line(k - half))
        cols_mine = jnp.concatenate([both, *got], axis=0)
        cols_theirs = lax.ppermute(cols_mine, AXES, other_core)

        x = dict(zip([half, 0], prepare_rows(scale, [points_of[half], points], 40)))
        x |= dict(zip(direct[:-1], prepare_rows(scale, [points_of[k] for k in direct[:-1]], 1)))
        ks = [0, *direct]
        part, mine = times_columns(scale, outputscale, noise, [cols_mine], [x[k] for k in ks], [], 20)
        total = dict(zip(ks, part))
        last = lax.optimization_barrier((*[points_of[k] for k in forwarded], *part))[: len(forwarded)]
        part, x_last = times_prepared(scale, last, [mine], 10)
        total |= dict(zip(forwarded, part))
        x |= dict(zip(forwarded, x_last))
        ks = [*forwarded, *direct[1:], 1]
        part, theirs = times_columns(scale, outputscale, noise, [cols_theirs], [x[k] for k in ks], [total[k] for k in ks], 10)
        total |= dict(zip(ks, part))
        total |= dict(zip([0], times_near(theirs, [x[0]], [total[0]], 10)))
        got = [
            lax.ppermute(total[k], AXES, [(b, a) for a, b in along_line(k)]) for k in [*direct[1:], *forwarded, 1]
        ]
        return add_most([total[0], *got[:-1]], 10) + got[-1]

    placed = (P(AXES, None), P(AXES, None), P(), P(), P())
    return jax.shard_map(per_device, mesh=mesh, in_specs=placed, out_specs=P(AXES, None), check_vma=False)
```

```python
import functools
import math

import jax
import jax.numpy as jnp
from jax import lax
from jax.experimental import pallas as pl
from jax.experimental.pallas import tpu as pltpu
from jax.sharding import PartitionSpec as P

AXES = ("outer", "inner")
CORES = 2
VMEM = pl.BlockSpec(memory_space=pltpu.VMEM)
BF16 = jnp.bfloat16
F32 = jnp.float32
LIMIT = 24 * 1024 * 1024
LANES = 128
LN2 = math.log(2.0)
GROUP = 4


def partner(index, step, size):
    return index ^ step if size & (size - 1) == 0 else (index + step) % size


def split(x):
    high = x.astype(BF16)
    return high, (x - high.astype(F32)).astype(BF16)


def cost(us):
    return pl.CostEstimate(flops=int(us * 1e9), bytes_accessed=1024, transcendentals=0)


def params():
    return pltpu.CompilerParams(vmem_limit_bytes=LIMIT)


def kernel_scale(scale_ref):
    return (math.sqrt(5.0) / LN2) / scale_ref[...]


def norm_lanes(norm, first):
    high, mid = split(norm)
    low = (norm - high.astype(F32) - mid.astype(F32)).astype(BF16)
    lane = lax.broadcasted_iota(jnp.int32, (norm.shape[0], LANES), 1)
    out = jnp.where((lane >= 3 - first) & (lane < 6 - first), 1.0, 0.0)
    for i, part in enumerate((high, mid, low)):
        out = jnp.where(lane == first + i, part.astype(F32), out)
    return out.astype(BF16)


def put(ref, at, parts):
    start = 0
    for part in parts:
        ref[at, start : start + part.shape[1]] = part
        start += part.shape[1]


def fill_rows(x_ref, at, block, scale):
    high, low = split(block * scale)
    x = high.astype(F32) + low.astype(F32)
    norm = jnp.sum(x * x, axis=1, keepdims=True)
    high, low = (-2.0 * high.astype(F32)).astype(BF16), (-2.0 * low.astype(F32)).astype(BF16)
    put(x_ref, at, (high, low, high, low, norm_lanes(norm, 0)))


def fill_cols(y_ref, v_ref, at, block, scale, amplitude):
    features = scale.shape[1]
    high, low = split(block[:, :features] * scale)
    y = high.astype(F32) + low.astype(F32)
    norm = jnp.sum(y * y, axis=1, keepdims=True)
    put(y_ref, at, (high, high, low, low, norm_lanes(norm, 3)))
    put(v_ref, at, split(block[:, features:] * (amplitude * LN2)))


def blank_kernel(out_ref):
    out_ref[...] = jnp.zeros_like(out_ref)


def blank(shape, us):
    return pl.pallas_call(
        blank_kernel,
        out_shape=jax.ShapeDtypeStruct(shape, F32),
        out_specs=VMEM,
        compiler_params=params(),
        cost_estimate=cost(us),
        name="blank",
    )()


def join_kernel(a_ref, b_ref, _, out_ref):
    put(out_ref, slice(None), (a_ref[...], b_ref[...]))


def join(a, b, out):
    return pl.pallas_call(
        join_kernel,
        out_shape=jax.ShapeDtypeStruct(out.shape, out.dtype),
        in_specs=[VMEM] * 3,
        out_specs=VMEM,
        input_output_aliases={2: 0},
        compiler_params=params(),
        cost_estimate=cost(1),
        name="join",
    )(a, b, out)


def rows_kernel(scale_ref, *refs):
    n = len(refs) // 2
    scale = kernel_scale(scale_ref)
    for block, x_ref in zip(refs[:n], refs[n:]):
        fill_rows(x_ref, slice(None), block[...], scale)


def prepare_rows(scale, blocks, us):
    here, features = blocks[0].shape
    return pl.pallas_call(
        rows_kernel,
        out_shape=[jax.ShapeDtypeStruct((here, 4 * features + LANES), BF16)] * len(blocks),
        in_specs=[VMEM] * (1 + len(blocks)),
        out_specs=[VMEM] * len(blocks),
        compiler_params=params(),
        cost_estimate=cost(us),
        name="rows",
    )(scale, *blocks)


def times_tile(x, y_ref, v_ref):
    columns = v_ref.shape[1] // 2
    b2 = lax.dot_general(x, y_ref[...], (((1,), (1,)), ((), ())), preferred_element_type=F32)
    b2 = jnp.maximum(b2, 1e-30)
    b = b2 * lax.rsqrt(b2)
    high, low = split((b2 * (LN2 / 3.0) + b + (1.0 / LN2)) * jnp.exp2(-b))
    total = jnp.dot(high, v_ref[...], preferred_element_type=F32)
    return total[:, :columns] + total[:, columns:] + jnp.dot(low, v_ref[:, :columns], preferred_element_type=F32)


def fill_all(cols, y_ref, v_ref, scale, amplitude):
    at = 0
    for block in cols:
        fill_cols(y_ref, v_ref, slice(at, at + block.shape[0]), block[...], scale, amplitude)
        at += block.shape[0]


def groups(n):
    return [range(first, min(first + GROUP, n)) for first in range(0, n, GROUP)]


def tile_kernel(n_cols, n_rows, scale_ref, amp_ref, noise_ref, *refs):
    cols, rows, rest = refs[:n_cols], refs[n_cols : n_cols + n_rows], refs[n_cols + n_rows :]
    starts, outs, (y_ref, v_ref) = rest[: -n_rows - 2], rest[-n_rows - 2 : -2], rest[-2:]
    here = rows[0].shape[0]
    fill_all(cols, y_ref, v_ref, kernel_scale(scale_ref), amp_ref[...])
    for group in groups(n_rows):
        total = times_tile(jnp.concatenate([rows[i][...] for i in group], axis=0), y_ref, v_ref)
        for j, i in enumerate(group):
            out = total[j * here : (j + 1) * here, :]
            if starts:
                out = out + starts[i][...]
            elif i == 0:
                out = out + noise_ref[...] * cols[0][:here, -out.shape[1] :]
            outs[i][...] = out


def prepared_shapes(cols, features):
    n, width = sum(block.shape[0] for block in cols), cols[0].shape[1]
    return [
        jax.ShapeDtypeStruct((n, 4 * features + LANES), BF16),
        jax.ShapeDtypeStruct((n, 2 * (width - features)), BF16),
    ]


def times_columns(scale, amplitude, noise, cols, rows, starts, us):
    here = rows[0].shape[0]
    features = scale.shape[1]
    given = [scale, amplitude[None, :], noise[None, :], *cols, *rows, *starts]
    *outs, y, v = pl.pallas_call(
        functools.partial(tile_kernel, len(cols), len(rows)),
        out_shape=[jax.ShapeDtypeStruct((here, cols[0].shape[1] - features), F32)] * len(rows)
        + prepared_shapes(cols, features),
        in_specs=[VMEM] * len(given),
        out_specs=[VMEM] * (len(rows) + 2),
        compiler_params=params(),
        cost_estimate=cost(us),
        name="tile",
    )(*given)
    return outs, (y, v)


def last_kernel(n_blocks, scale_ref, *refs):
    blocks, prepared, outs, xs = refs[:n_blocks], refs[n_blocks : -2 * n_blocks], refs[-2 * n_blocks : -n_blocks], refs[-n_blocks:]
    scale = kernel_scale(scale_ref)
    here = blocks[0].shape[0]
    for block, x_ref in zip(blocks, xs):
        fill_rows(x_ref, slice(None), block[...], scale)
    for group in groups(n_blocks):
        x = jnp.concatenate([xs[i][...] for i in group], axis=0)
        total = times_tile(x, *prepared)
        for j, i in enumerate(group):
            outs[i][...] = total[j * here : (j + 1) * here, :]


def times_prepared(scale, blocks, prepared, us):
    n = len(blocks)
    here, features = blocks[0].shape
    columns = prepared[0][1].shape[1] // 2
    given = [scale, *blocks, *prepared[0]]
    out = pl.pallas_call(
        functools.partial(last_kernel, n),
        out_shape=[jax.ShapeDtypeStruct((here, columns), F32)] * n
        + [jax.ShapeDtypeStruct((here, 4 * features + LANES), BF16)] * n,
        in_specs=[VMEM] * len(given),
        out_specs=[VMEM] * (2 * n),
        compiler_params=params(),
        cost_estimate=cost(us),
        name="last",
    )(*given)
    return out[:n], out[n:]


def near_kernel(y_ref, v_ref, *refs):
    n = len(refs) // 3
    rows, starts, outs = refs[:n], refs[n : 2 * n], refs[2 * n :]
    here = rows[0].shape[0]
    total = times_tile(jnp.concatenate([row[...] for row in rows], axis=0), y_ref, v_ref)
    for i in range(n):
        outs[i][...] = starts[i][...] + total[i * here : (i + 1) * here, :]


def times_near(prepared, rows, starts, us):
    return pl.pallas_call(
        near_kernel,
        out_shape=[jax.ShapeDtypeStruct(start.shape, F32) for start in starts],
        in_specs=[VMEM] * (2 + 2 * len(rows)),
        out_specs=[VMEM] * len(rows),
        compiler_params=params(),
        cost_estimate=cost(us),
        name="near",
    )(*prepared, *rows, *starts)


def add_kernel(*refs):
    out = refs[0][...]
    for ref in refs[1:-1]:
        out = out + ref[...]
    refs[-1][...] = out


def add_most(parts, us):
    return pl.pallas_call(
        add_kernel,
        out_shape=jax.ShapeDtypeStruct(parts[0].shape, F32),
        in_specs=[VMEM] * len(parts),
        out_specs=VMEM,
        compiler_params=params(),
        cost_estimate=cost(us),
        name="add",
    )(*parts)


def solution(mesh):
    n_outer, n_inner = mesh.shape["outer"], mesh.shape["inner"]
    n_line = n_inner // CORES

    def linear(outer, line, core):
        return outer * n_inner + line * CORES + core

    places = [(o, z, c) for o in range(n_outer) for z in range(n_line) for c in range(CORES)]

    def along_line(step):
        return [(linear(o, z, c), linear(o, partner(z, step, n_line), c)) for o, z, c in places]

    def along_outer(step):
        return [(linear(o, z, c), linear(partner(o, step, n_outer), z, c)) for o, z, c in places]

    other_core = [(linear(o, z, c), linear(o, z, c ^ 1)) for o, z, c in places]

    def per_device(points, vectors, lengthscales, outputscale, noise):
        scale = lengthscales[None, :]
        half = n_line // 2
        direct = list(range(1, half + 1))
        forwarded = list(range(half + 1, n_line))
        points_of = {half: lax.ppermute(points, AXES, along_line(half))}
        here, features = points.shape
        both = blank((here, features + vectors.shape[1]), 20)
        both = join(points, vectors, both)
        got = [lax.ppermute(both, AXES, along_outer(k)) for k in [n_outer - 1, *range(1, n_outer - 1)]]
        for k in direct[:-1]:
            points_of[k] = lax.ppermute(points, AXES, along_line(k))
        for k in forwarded:
            points_of[k] = lax.ppermute(points_of[half], AXES, along_line(k - half))
        cols_mine = jnp.concatenate([both, *got], axis=0)
        cols_theirs = lax.ppermute(cols_mine, AXES, other_core)

        x = dict(zip([half, 0], prepare_rows(scale, [points_of[half], points], 40)))
        x |= dict(zip(direct[:-1], prepare_rows(scale, [points_of[k] for k in direct[:-1]], 1)))
        ks = [0, *direct]
        part, mine = times_columns(scale, outputscale, noise, [cols_mine], [x[k] for k in ks], [], 20)
        total = dict(zip(ks, part))
        last = lax.optimization_barrier((*[points_of[k] for k in forwarded], *part))[: len(forwarded)]
        part, x_last = times_prepared(scale, last, [mine], 10)
        total |= dict(zip(forwarded, part))
        x |= dict(zip(forwarded, x_last))
        ks = [*forwarded, *direct[1:], 1]
        part, theirs = times_columns(scale, outputscale, noise, [cols_theirs], [x[k] for k in ks], [total[k] for k in ks], 10)
        total |= dict(zip(ks, part))
        total |= dict(zip([0], times_near(theirs, [x[0]], [total[0]], 10)))
        got = [
            lax.ppermute(total[k], AXES, [(b, a) for a, b in along_line(k)]) for k in [*direct[1:], *forwarded, 1]
        ]
        return add_most([total[0], *got[:-1]], 10) + got[-1]

    placed = (P(AXES, None), P(AXES, None), P(), P(), P())
    return jax.shard_map(per_device, mesh=mesh, in_specs=placed, out_specs=P(AXES, None), check_vma=False)
```

```python
import functools
import math

import jax
import jax.numpy as jnp
from jax import lax
from jax.experimental import pallas as pl
from jax.experimental.pallas import tpu as pltpu
from jax.sharding import PartitionSpec as P

AXES = ("outer", "inner")
CORES = 2
VMEM = pl.BlockSpec(memory_space=pltpu.VMEM)
BF16 = jnp.bfloat16
F32 = jnp.float32
LIMIT = 24 * 1024 * 1024
LANES = 128
LN2 = math.log(2.0)
GROUP = 4


def partner(index, step, size):
    return index ^ step if size & (size - 1) == 0 else (index + step) % size


def split(x):
    high = x.astype(BF16)
    return high, (x - high.astype(F32)).astype(BF16)


def cost(us):
    return pl.CostEstimate(flops=int(us * 1e9), bytes_accessed=1024, transcendentals=0)


def params():
    return pltpu.CompilerParams(vmem_limit_bytes=LIMIT)


def kernel_scale(scale_ref):
    return (math.sqrt(5.0) / LN2) / scale_ref[...]


def norm_lanes(norm, first):
    high, mid = split(norm)
    low = (norm - high.astype(F32) - mid.astype(F32)).astype(BF16)
    lane = lax.broadcasted_iota(jnp.int32, (norm.shape[0], LANES), 1)
    out = jnp.where((lane >= 3 - first) & (lane < 6 - first), 1.0, 0.0)
    for i, part in enumerate((high, mid, low)):
        out = jnp.where(lane == first + i, part.astype(F32), out)
    return out.astype(BF16)


def put(ref, at, parts):
    start = 0
    for part in parts:
        ref[at, start : start + part.shape[1]] = part
        start += part.shape[1]


def fill_rows(x_ref, at, block, scale):
    high, low = split(block * scale)
    x = high.astype(F32) + low.astype(F32)
    norm = jnp.sum(x * x, axis=1, keepdims=True)
    high, low = (-2.0 * high.astype(F32)).astype(BF16), (-2.0 * low.astype(F32)).astype(BF16)
    put(x_ref, at, (high, low, high, low, norm_lanes(norm, 0)))


def fill_cols(y_ref, v_ref, at, block, scale, amplitude):
    features = scale.shape[1]
    high, low = split(block[:, :features] * scale)
    y = high.astype(F32) + low.astype(F32)
    norm = jnp.sum(y * y, axis=1, keepdims=True)
    put(y_ref, at, (high, high, low, low, norm_lanes(norm, 3)))
    put(v_ref, at, split(block[:, features:] * (amplitude * LN2)))


def blank_kernel(out_ref):
    out_ref[...] = jnp.zeros_like(out_ref)


def blank(shape, us):
    return pl.pallas_call(
        blank_kernel,
        out_shape=jax.ShapeDtypeStruct(shape, F32),
        out_specs=VMEM,
        compiler_params=params(),
        cost_estimate=cost(us),
        name="blank",
    )()


def join_kernel(a_ref, b_ref, _, out_ref):
    put(out_ref, slice(None), (a_ref[...], b_ref[...]))


def join(a, b, out):
    return pl.pallas_call(
        join_kernel,
        out_shape=jax.ShapeDtypeStruct(out.shape, out.dtype),
        in_specs=[VMEM] * 3,
        out_specs=VMEM,
        input_output_aliases={2: 0},
        compiler_params=params(),
        cost_estimate=cost(1),
        name="join",
    )(a, b, out)


def rows_kernel(scale_ref, *refs):
    n = len(refs) // 2
    scale = kernel_scale(scale_ref)
    for block, x_ref in zip(refs[:n], refs[n:]):
        fill_rows(x_ref, slice(None), block[...], scale)


def prepare_rows(scale, blocks, us):
    here, features = blocks[0].shape
    return pl.pallas_call(
        rows_kernel,
        out_shape=[jax.ShapeDtypeStruct((here, 4 * features + LANES), BF16)] * len(blocks),
        in_specs=[VMEM] * (1 + len(blocks)),
        out_specs=[VMEM] * len(blocks),
        compiler_params=params(),
        cost_estimate=cost(us),
        name="rows",
    )(scale, *blocks)


def times_tile(x, y_ref, v_ref):
    columns = v_ref.shape[1] // 2
    b2 = lax.dot_general(x, y_ref[...], (((1,), (1,)), ((), ())), preferred_element_type=F32)
    b2 = jnp.maximum(b2, 1e-30)
    b = b2 * lax.rsqrt(b2)
    high, low = split((b2 * (LN2 / 3.0) + b + (1.0 / LN2)) * jnp.exp2(-b))
    total = jnp.dot(high, v_ref[...], preferred_element_type=F32)
    return total[:, :columns] + total[:, columns:] + jnp.dot(low, v_ref[:, :columns], preferred_element_type=F32)


def fill_all(cols, y_ref, v_ref, scale, amplitude):
    at = 0
    for block in cols:
        fill_cols(y_ref, v_ref, slice(at, at + block.shape[0]), block[...], scale, amplitude)
        at += block.shape[0]


def groups(n):
    return [range(first, min(first + GROUP, n)) for first in range(0, n, GROUP)]


def tile_kernel(n_cols, n_rows, scale_ref, amp_ref, noise_ref, *refs):
    cols, rows, rest = refs[:n_cols], refs[n_cols : n_cols + n_rows], refs[n_cols + n_rows :]
    starts, outs, (y_ref, v_ref) = rest[: -n_rows - 2], rest[-n_rows - 2 : -2], rest[-2:]
    here = rows[0].shape[0]
    fill_all(cols, y_ref, v_ref, kernel_scale(scale_ref), amp_ref[...])
    for group in groups(n_rows):
        total = times_tile(jnp.concatenate([rows[i][...] for i in group], axis=0), y_ref, v_ref)
        for j, i in enumerate(group):
            out = total[j * here : (j + 1) * here, :]
            if starts:
                out = out + starts[i][...]
            elif i == 0:
                out = out + noise_ref[...] * cols[0][:here, -out.shape[1] :]
            outs[i][...] = out


def prepared_shapes(cols, features):
    n, width = sum(block.shape[0] for block in cols), cols[0].shape[1]
    return [
        jax.ShapeDtypeStruct((n, 4 * features + LANES), BF16),
        jax.ShapeDtypeStruct((n, 2 * (width - features)), BF16),
    ]


def times_columns(scale, amplitude, noise, cols, rows, starts, us):
    here = rows[0].shape[0]
    features = scale.shape[1]
    given = [scale, amplitude[None, :], noise[None, :], *cols, *rows, *starts]
    *outs, y, v = pl.pallas_call(
        functools.partial(tile_kernel, len(cols), len(rows)),
        out_shape=[jax.ShapeDtypeStruct((here, cols[0].shape[1] - features), F32)] * len(rows)
        + prepared_shapes(cols, features),
        in_specs=[VMEM] * len(given),
        out_specs=[VMEM] * (len(rows) + 2),
        compiler_params=params(),
        cost_estimate=cost(us),
        name="tile",
    )(*given)
    return outs, (y, v)


def last_kernel(n_blocks, scale_ref, *refs):
    blocks, prepared, outs, xs = refs[:n_blocks], refs[n_blocks : -2 * n_blocks], refs[-2 * n_blocks : -n_blocks], refs[-n_blocks:]
    scale = kernel_scale(scale_ref)
    here = blocks[0].shape[0]
    for block, x_ref in zip(blocks, xs):
        fill_rows(x_ref, slice(None), block[...], scale)
    for group in groups(n_blocks):
        x = jnp.concatenate([xs[i][...] for i in group], axis=0)
        total = times_tile(x, *prepared)
        for j, i in enumerate(group):
            outs[i][...] = total[j * here : (j + 1) * here, :]


def times_prepared(scale, blocks, prepared, us):
    n = len(blocks)
    here, features = blocks[0].shape
    columns = prepared[0][1].shape[1] // 2
    given = [scale, *blocks, *prepared[0]]
    out = pl.pallas_call(
        functools.partial(last_kernel, n),
        out_shape=[jax.ShapeDtypeStruct((here, columns), F32)] * n
        + [jax.ShapeDtypeStruct((here, 4 * features + LANES), BF16)] * n,
        in_specs=[VMEM] * len(given),
        out_specs=[VMEM] * (2 * n),
        compiler_params=params(),
        cost_estimate=cost(us),
        name="last",
    )(*given)
    return out[:n], out[n:]


def near_kernel(y_ref, v_ref, *refs):
    n = len(refs) // 3
    rows, starts, outs = refs[:n], refs[n : 2 * n], refs[2 * n :]
    here = rows[0].shape[0]
    total = times_tile(jnp.concatenate([row[...] for row in rows], axis=0), y_ref, v_ref)
    for i in range(n):
        outs[i][...] = starts[i][...] + total[i * here : (i + 1) * here, :]


def times_near(prepared, rows, starts, us):
    return pl.pallas_call(
        near_kernel,
        out_shape=[jax.ShapeDtypeStruct(start.shape, F32) for start in starts],
        in_specs=[VMEM] * (2 + 2 * len(rows)),
        out_specs=[VMEM] * len(rows),
        compiler_params=params(),
        cost_estimate=cost(us),
        name="near",
    )(*prepared, *rows, *starts)


def solution(mesh):
    n_outer, n_inner = mesh.shape["outer"], mesh.shape["inner"]
    n_line = n_inner // CORES

    def linear(outer, line, core):
        return outer * n_inner + line * CORES + core

    places = [(o, z, c) for o in range(n_outer) for z in range(n_line) for c in range(CORES)]

    def along_line(step):
        return [(linear(o, z, c), linear(o, partner(z, step, n_line), c)) for o, z, c in places]

    def along_outer(step):
        return [(linear(o, z, c), linear(partner(o, step, n_outer), z, c)) for o, z, c in places]

    other_core = [(linear(o, z, c), linear(o, z, c ^ 1)) for o, z, c in places]

    def per_device(points, vectors, lengthscales, outputscale, noise):
        scale = lengthscales[None, :]
        half = n_line // 2
        direct = list(range(1, half + 1))
        forwarded = list(range(half + 1, n_line))
        points_of = {half: lax.ppermute(points, AXES, along_line(half))}
        here, features = points.shape
        both = blank((here, features + vectors.shape[1]), 20)
        both = join(points, vectors, both)
        got = [lax.ppermute(both, AXES, along_outer(k)) for k in [n_outer - 1, *range(1, n_outer - 1)]]
        for k in direct[:-1]:
            points_of[k] = lax.ppermute(points, AXES, along_line(k))
        for k in forwarded:
            points_of[k] = lax.ppermute(points_of[half], AXES, along_line(k - half))
        cols_mine = jnp.concatenate([both, *got], axis=0)
        cols_theirs = lax.ppermute(cols_mine, AXES, other_core)

        x = dict(zip([half, 0], prepare_rows(scale, [points_of[half], points], 40)))
        x |= dict(zip(direct[:-1], prepare_rows(scale, [points_of[k] for k in direct[:-1]], 1)))
        ks = [0, *direct]
        part, mine = times_columns(scale, outputscale, noise, [cols_mine], [x[k] for k in ks], [], 20)
        total = dict(zip(ks, part))
        last = lax.optimization_barrier((*[points_of[k] for k in forwarded], *part))[: len(forwarded)]
        part, x_last = times_prepared(scale, last, [mine], 10)
        total |= dict(zip(forwarded, part))
        x |= dict(zip(forwarded, x_last))
        ks = [*forwarded, *direct[1:], 1]
        part, theirs = times_columns(scale, outputscale, noise, [cols_theirs], [x[k] for k in ks], [total[k] for k in ks], 10)
        total |= dict(zip(ks, part))
        total |= dict(zip([0], times_near(theirs, [x[0]], [total[0]], 10)))
        got = [
            lax.ppermute(total[k], AXES, [(b, a) for a, b in along_line(k)]) for k in [*direct[1:], *forwarded, 1]
        ]
        return sum(got, total[0])

    placed = (P(AXES, None), P(AXES, None), P(), P(), P())
    return jax.shard_map(per_device, mesh=mesh, in_specs=placed, out_specs=P(AXES, None), check_vma=False)
```

```python
import functools
import math

import jax
import jax.numpy as jnp
from jax import lax
from jax.experimental import pallas as pl
from jax.experimental.pallas import tpu as pltpu
from jax.sharding import PartitionSpec as P

AXES = ("outer", "inner")
CORES = 2
VMEM = pl.BlockSpec(memory_space=pltpu.VMEM)
BF16 = jnp.bfloat16
F32 = jnp.float32
LIMIT = 24 * 1024 * 1024
LANES = 128
LN2 = math.log(2.0)
GROUP = 4


def partner(index, step, size):
    return index ^ step if size & (size - 1) == 0 else (index + step) % size


def split(x):
    high = x.astype(BF16)
    return high, (x - high.astype(F32)).astype(BF16)


def cost(us):
    return pl.CostEstimate(flops=int(us * 1e9), bytes_accessed=1024, transcendentals=0)


def params():
    return pltpu.CompilerParams(vmem_limit_bytes=LIMIT)


def kernel_scale(scale_ref):
    return (math.sqrt(5.0) / LN2) / scale_ref[...]


def norm_lanes(norm, first):
    high, mid = split(norm)
    low = (norm - high.astype(F32) - mid.astype(F32)).astype(BF16)
    lane = lax.broadcasted_iota(jnp.int32, (norm.shape[0], LANES), 1)
    out = jnp.where((lane >= 3 - first) & (lane < 6 - first), 1.0, 0.0)
    for i, part in enumerate((high, mid, low)):
        out = jnp.where(lane == first + i, part.astype(F32), out)
    return out.astype(BF16)


def put(ref, at, parts):
    start = 0
    for part in parts:
        ref[at, start : start + part.shape[1]] = part
        start += part.shape[1]


def fill_rows(x_ref, at, block, scale):
    high, low = split(block * scale)
    x = high.astype(F32) + low.astype(F32)
    norm = jnp.sum(x * x, axis=1, keepdims=True)
    high, low = (-2.0 * high.astype(F32)).astype(BF16), (-2.0 * low.astype(F32)).astype(BF16)
    put(x_ref, at, (high, low, high, low, norm_lanes(norm, 0)))


def fill_cols(y_ref, v_ref, at, block, scale, amplitude):
    features = scale.shape[1]
    high, low = split(block[:, :features] * scale)
    y = high.astype(F32) + low.astype(F32)
    norm = jnp.sum(y * y, axis=1, keepdims=True)
    put(y_ref, at, (high, high, low, low, norm_lanes(norm, 3)))
    put(v_ref, at, split(block[:, features:] * (amplitude * LN2)))


def blank_kernel(out_ref):
    out_ref[...] = jnp.zeros_like(out_ref)


def blank(shape, us):
    return pl.pallas_call(
        blank_kernel,
        out_shape=jax.ShapeDtypeStruct(shape, F32),
        out_specs=VMEM,
        compiler_params=params(),
        cost_estimate=cost(us),
        name="blank",
    )()


def join_kernel(a_ref, b_ref, _, out_ref):
    put(out_ref, slice(None), (a_ref[...], b_ref[...]))


def join(a, b, out):
    return pl.pallas_call(
        join_kernel,
        out_shape=jax.ShapeDtypeStruct(out.shape, out.dtype),
        in_specs=[VMEM] * 3,
        out_specs=VMEM,
        input_output_aliases={2: 0},
        compiler_params=params(),
        cost_estimate=cost(1),
        name="join",
    )(a, b, out)


def rows_kernel(scale_ref, *refs):
    n = len(refs) // 2
    scale = kernel_scale(scale_ref)
    for block, x_ref in zip(refs[:n], refs[n:]):
        fill_rows(x_ref, slice(None), block[...], scale)


def prepare_rows(scale, blocks, us):
    here, features = blocks[0].shape
    return pl.pallas_call(
        rows_kernel,
        out_shape=[jax.ShapeDtypeStruct((here, 4 * features + LANES), BF16)] * len(blocks),
        in_specs=[VMEM] * (1 + len(blocks)),
        out_specs=[VMEM] * len(blocks),
        compiler_params=params(),
        cost_estimate=cost(us),
        name="rows",
    )(scale, *blocks)


def times_tile(x, y_ref, v_ref):
    columns = v_ref.shape[1] // 2
    b2 = lax.dot_general(x, y_ref[...], (((1,), (1,)), ((), ())), preferred_element_type=F32)
    b2 = jnp.maximum(b2, 1e-30)
    b = b2 * lax.rsqrt(b2)
    high, low = split((b2 * (LN2 / 3.0) + b + (1.0 / LN2)) * jnp.exp2(-b))
    total = jnp.dot(high, v_ref[...], preferred_element_type=F32)
    return total[:, :columns] + total[:, columns:] + jnp.dot(low, v_ref[:, :columns], preferred_element_type=F32)


def fill_all(cols, y_ref, v_ref, scale, amplitude):
    at = 0
    for block in cols:
        fill_cols(y_ref, v_ref, slice(at, at + block.shape[0]), block[...], scale, amplitude)
        at += block.shape[0]


def groups(n):
    return [range(first, min(first + GROUP, n)) for first in range(0, n, GROUP)]


def tile_kernel(n_cols, n_rows, scale_ref, amp_ref, noise_ref, *refs):
    cols, rows, rest = refs[:n_cols], refs[n_cols : n_cols + n_rows], refs[n_cols + n_rows :]
    starts, outs, (y_ref, v_ref) = rest[: -n_rows - 2], rest[-n_rows - 2 : -2], rest[-2:]
    here = rows[0].shape[0]
    fill_all(cols, y_ref, v_ref, kernel_scale(scale_ref), amp_ref[...])
    for group in groups(n_rows):
        total = times_tile(jnp.concatenate([rows[i][...] for i in group], axis=0), y_ref, v_ref)
        for j, i in enumerate(group):
            out = total[j * here : (j + 1) * here, :]
            if starts:
                out = out + starts[i][...]
            elif i == 0:
                out = out + noise_ref[...] * cols[0][:here, -out.shape[1] :]
            outs[i][...] = out


def prepared_shapes(cols, features):
    n, width = sum(block.shape[0] for block in cols), cols[0].shape[1]
    return [
        jax.ShapeDtypeStruct((n, 4 * features + LANES), BF16),
        jax.ShapeDtypeStruct((n, 2 * (width - features)), BF16),
    ]


def times_columns(scale, amplitude, noise, cols, rows, starts, us):
    here = rows[0].shape[0]
    features = scale.shape[1]
    given = [scale, amplitude[None, :], noise[None, :], *cols, *rows, *starts]
    *outs, y, v = pl.pallas_call(
        functools.partial(tile_kernel, len(cols), len(rows)),
        out_shape=[jax.ShapeDtypeStruct((here, cols[0].shape[1] - features), F32)] * len(rows)
        + prepared_shapes(cols, features),
        in_specs=[VMEM] * len(given),
        out_specs=[VMEM] * (len(rows) + 2),
        compiler_params=params(),
        cost_estimate=cost(us),
        name="tile",
    )(*given)
    return outs, (y, v)


def last_kernel(n_blocks, scale_ref, *refs):
    blocks, prepared, outs, xs = refs[:n_blocks], refs[n_blocks : -2 * n_blocks], refs[-2 * n_blocks : -n_blocks], refs[-n_blocks:]
    scale = kernel_scale(scale_ref)
    here = blocks[0].shape[0]
    for block, x_ref in zip(blocks, xs):
        fill_rows(x_ref, slice(None), block[...], scale)
    for group in groups(n_blocks):
        x = jnp.concatenate([xs[i][...] for i in group], axis=0)
        total = times_tile(x, *prepared)
        for j, i in enumerate(group):
            outs[i][...] = total[j * here : (j + 1) * here, :]


def times_prepared(scale, blocks, prepared, us):
    n = len(blocks)
    here, features = blocks[0].shape
    columns = prepared[0][1].shape[1] // 2
    given = [scale, *blocks, *prepared[0]]
    out = pl.pallas_call(
        functools.partial(last_kernel, n),
        out_shape=[jax.ShapeDtypeStruct((here, columns), F32)] * n
        + [jax.ShapeDtypeStruct((here, 4 * features + LANES), BF16)] * n,
        in_specs=[VMEM] * len(given),
        out_specs=[VMEM] * (2 * n),
        compiler_params=params(),
        cost_estimate=cost(us),
        name="last",
    )(*given)
    return out[:n], out[n:]


def near_kernel(y_ref, v_ref, *refs):
    n = len(refs) // 3
    rows, starts, outs = refs[:n], refs[n : 2 * n], refs[2 * n :]
    here = rows[0].shape[0]
    total = times_tile(jnp.concatenate([row[...] for row in rows], axis=0), y_ref, v_ref)
    for i in range(n):
        outs[i][...] = starts[i][...] + total[i * here : (i + 1) * here, :]


def times_near(prepared, rows, starts, us):
    return pl.pallas_call(
        near_kernel,
        out_shape=[jax.ShapeDtypeStruct(start.shape, F32) for start in starts],
        in_specs=[VMEM] * (2 + 2 * len(rows)),
        out_specs=[VMEM] * len(rows),
        compiler_params=params(),
        cost_estimate=cost(us),
        name="near",
    )(*prepared, *rows, *starts)


def solution(mesh):
    n_outer, n_inner = mesh.shape["outer"], mesh.shape["inner"]
    n_line = n_inner // CORES

    def linear(outer, line, core):
        return outer * n_inner + line * CORES + core

    places = [(o, z, c) for o in range(n_outer) for z in range(n_line) for c in range(CORES)]

    def along_line(step):
        return [(linear(o, z, c), linear(o, partner(z, step, n_line), c)) for o, z, c in places]

    def along_outer(step):
        return [(linear(o, z, c), linear(partner(o, step, n_outer), z, c)) for o, z, c in places]

    other_core = [(linear(o, z, c), linear(o, z, c ^ 1)) for o, z, c in places]

    def per_device(points, vectors, lengthscales, outputscale, noise):
        scale = lengthscales[None, :]
        half = n_line // 2
        direct = list(range(1, half + 1))
        forwarded = list(range(half + 1, n_line))
        points_of = {half: lax.ppermute(points, AXES, along_line(half))}
        here, features = points.shape
        both = blank((here, features + vectors.shape[1]), 20)
        both = join(points, vectors, both)
        got = [lax.ppermute(both, AXES, along_outer(k)) for k in [n_outer - 1, *range(1, n_outer - 1)]]
        for k in direct[:-1]:
            points_of[k] = lax.ppermute(points, AXES, along_line(k))
        for k in forwarded:
            points_of[k] = lax.ppermute(points_of[half], AXES, along_line(k - half))
        cols_mine = jnp.concatenate([both, *got], axis=0)
        cols_theirs = lax.ppermute(cols_mine, AXES, other_core)

        x = dict(zip([half, 0], prepare_rows(scale, [points_of[half], points], 40)))
        x |= dict(zip(direct[:-1], prepare_rows(scale, [points_of[k] for k in direct[:-1]], 8)))
        ks = [0, *direct]
        part, mine = times_columns(scale, outputscale, noise, [cols_mine], [x[k] for k in ks], [], 20)
        total = dict(zip(ks, part))
        last = lax.optimization_barrier((*[points_of[k] for k in forwarded], *part))[: len(forwarded)]
        part, x_last = times_prepared(scale, last, [mine], 10)
        total |= dict(zip(forwarded, part))
        x |= dict(zip(forwarded, x_last))
        ks = [*forwarded, *direct[1:], 1]
        part, theirs = times_columns(scale, outputscale, noise, [cols_theirs], [x[k] for k in ks], [total[k] for k in ks], 10)
        total |= dict(zip(ks, part))
        total |= dict(zip([0], times_near(theirs, [x[0]], [total[0]], 10)))
        got = [
            lax.ppermute(total[k], AXES, [(b, a) for a, b in along_line(k)]) for k in [*direct[1:], *forwarded, 1]
        ]
        return sum(got, total[0])

    placed = (P(AXES, None), P(AXES, None), P(), P(), P())
    return jax.shard_map(per_device, mesh=mesh, in_specs=placed, out_specs=P(AXES, None), check_vma=False)
```
